512 devices in a mesh: list: 16 (over z, core), sub: 8 (over y), slab: 4 (over x).
Axes of the slice: x: 4, y: 8, z: 8, core: 2. Of those that a mesh axis runs over, the one named last changes fastest.
Arguments:
- vectors: float32 [1024, 65536], P(None, ('list', 'sub', 'slab')), may hold values from -10 to 10
- centroids: bfloat16 [1024, 262144], P('sub', ('list', 'slab')), may hold values from -3 to 3
- codebook: float32 [32, 256, 32], P('sub'), may hold values from -10 to 10
- list_ids: int32 [65536], P(('list', 'sub', 'slab')), may hold values from 0 to 262143, as said below
Outputs:
- fresh_codebook: float32 [32, 256, 32], P('sub')
The draws below stay inside these ranges and needn't reach their ends.
Inputs may be any that keep to these rules, and one draw needn't show every extreme that they name: `list_ids`: among the columns of one device, at most 4 name lists of one owner (list id // 4096); in every draw one owner receives exactly 4 from every device.
All inputs are finite; a program needn't handle non-finite values.
Results may differ from the reference program's by a relative error of at most 0.0003.
Values sent between devices are 32-bit elements; how exact they have to be, the bound alone decides.
A program may use at most 64 MiB of HBM per device.

```python
import math
import jax
import jax.numpy as jnp
from jax import lax

D = 1024
SUBS = 32
CODES = 256
LISTS_DEV = 4096
ROWS_DEV = 128
SUBDIM = 32
LISTS = 262144
NV = 65536
N_LIST = 16
N_SLAB = 4


def draw_list_ids(key, part):
    owners = N_LIST * N_SLAB
    capacity = 2 * ROWS_DEV // owners
    blocks = NV // ROWS_DEV
    slot_count = owners * capacity
    base = jax.random.fold_in(key, 7001)
    key_hot, key_bias, key_noise, key_order, key_within = jax.random.split(base, 5)
    hottest = jax.random.randint(key_hot, (), 0, owners)
    owner_bias = jax.random.randint(key_bias, (blocks, owners), 0, 4)
    owner_bias = jnp.where(jnp.arange(owners)[None, :] == hottest, 7, owner_bias)
    slot_owner = jnp.arange(slot_count) // capacity
    slot_bias = owner_bias[:, slot_owner]
    noise = jax.random.randint(key_noise, (blocks, slot_count), 0, 2 ** 15)
    scores = (slot_bias * 2 ** 15 + noise) * slot_count + jnp.arange(slot_count)[None, :]
    unused, chosen = lax.top_k(scores, ROWS_DEV)
    shuffle = jax.random.randint(key_order, (blocks, ROWS_DEV), 0, 2 ** 20) * ROWS_DEV + jnp.arange(ROWS_DEV)[None, :]
    order = jnp.argsort(shuffle, axis=1)
    chosen = jnp.take_along_axis(chosen, order, axis=1)
    owner_of = chosen // capacity
    within = jax.random.randint(key_within, (blocks, ROWS_DEV), 0, LISTS_DEV)
    return (owner_of * LISTS_DEV + within).reshape(-1).astype(jnp.int32)


def draw_codebook(key, part):
    draw_key = jax.random.fold_in(key, 2718)
    background = jnp.clip(jax.random.normal(draw_key, (SUBS, CODES, SUBDIM), jnp.float32), -6.0, 6.0)
    return background


def draw_vectors(key, part):
    draw_key = jax.random.fold_in(key, 3141)
    result = jnp.clip(jax.random.normal(draw_key, (D, NV), jnp.float32), -6.0, 6.0)
    return result


def levels(stream_key, dims, shards, smallest, high):
    gain, own = 1.0, jax.random.fold_in(stream_key, 6)
    for dim, parts in shards:
        draws = jnp.exp(jax.random.uniform(jax.random.fold_in(own, dim), (parts,), jnp.float32, smallest / len(shards), high / len(shards)))
        gain = gain * jnp.repeat(draws, dims[dim] // parts).reshape([-1 if axis == dim else 1 for axis in range(len(dims))])
    return gain


def gaussian(rng, shape, scale, reach, shards=(), dtype=jnp.bfloat16):
    level = levels(rng, shape, shards, -0.22, 0.18) if shards else 1.0
    values = jax.random.normal(rng, shape, jnp.float32) * scale * level
    return jnp.minimum(jnp.maximum(values, -reach), reach).astype(dtype)


def setup_inputs(seed: int = 0) -> dict:
    key_of = jax.random.split(jax.random.key(seed), 5)
    vectors = draw_vectors(jax.random.fold_in(key_of[4], 71), 0)
    centroids = gaussian(key_of[1], (D, LISTS), 0.5, 3.0, ((0, 8), (1, 64)))
    codebook = draw_codebook(jax.random.fold_in(key_of[4], 71), 0)
    list_ids = draw_list_ids(jax.random.fold_in(key_of[4], 71), 0)
    return dict(vectors=vectors, centroids=centroids, codebook=codebook, list_ids=list_ids)


SOFTMAX_HEAT = 8.0
PRIOR_MASS = 1.0


def reference(vectors, centroids, codebook, list_ids):
    groups, num_codes, width = codebook.shape
    total_columns = vectors.shape[1]
    block = math.gcd(total_columns, 1024)
    codeword_norm = jnp.sum(codebook * codebook, axis=-1)

    def block_step(loop_index, running):
        counts, weighted = running
        offset = (loop_index * block).astype(jnp.int32)
        column_piece = lax.dynamic_slice_in_dim(vectors, offset, block, 1)
        list_rows = lax.dynamic_slice_in_dim(list_ids, offset, block, 0)
        nearest = jnp.take(centroids, list_rows, axis=1).astype(jnp.float32)
        residual = (column_piece - nearest).reshape(groups, width, block)
        inner_products = jnp.einsum("skd,sdn->skn", codebook, residual, precision=lax.Precision.HIGHEST)
        assignment_scores = (2.0 * inner_products - codeword_norm[:, :, None]) / SOFTMAX_HEAT
        assignment_scores = assignment_scores - jnp.max(assignment_scores, axis=1, keepdims=True)
        exponent = jnp.exp(assignment_scores)
        assign = exponent / jnp.sum(exponent, axis=1, keepdims=True)
        counts = counts + jnp.sum(assign, axis=2)
        weighted = weighted + jnp.einsum("skn,sdn->skd", assign, residual, precision=lax.Precision.HIGHEST)
        return counts, weighted

    start_state = (jnp.zeros((groups, num_codes), jnp.float32), jnp.zeros((groups, num_codes, width), jnp.float32))
    counts, weighted = lax.fori_loop(0, total_columns // block, block_step, start_state)
    return (weighted + PRIOR_MASS * codebook) / (counts[:, :, None] + PRIOR_MASS)
```

```python
import functools
import math

import jax
import jax.numpy as jnp
from jax import lax
from jax.experimental import pallas as pl
from jax.experimental.pallas import tpu as pltpu
from jax.sharding import PartitionSpec as P

SOFTMAX_HEAT = 8.0
PRIOR_MASS = 1.0
MESH = pl.DeviceIdType.MESH
F32, BF16, I32 = jnp.float32, jnp.bfloat16, jnp.int32
CAP = 4


def split3(x):
    a = x.astype(BF16)
    rest = x - a.astype(F32)
    b = rest.astype(BF16)
    c = (rest - b.astype(F32)).astype(BF16)
    return a, b, c


def dot(a, b, ca=1, cb=0):
    return lax.dot_general(a, b, (((ca,), (cb,)), ((), ())), preferred_element_type=F32)


def iota(shape, dim):
    return lax.broadcasted_iota(I32, shape, dim)


def kernel(
    dims,
    ids_ref, vec_ref, cen_ref, cb_ref,
    out_ref,
    cen_v, cb_v, ybuf, idbuf, slotbuf, send, recv, labsend, labrecv, labrow, cent, cbk, cbp, acc,
    arsend, arrecv, finsend, finrecv,
    lsem, ysend, yrecv, isend, irecv, labs, labr, dsend, drecv, rss, rsr, ags, agr,
):
    n_list, n_sub, n_slab, n_lists, cols, groups, codes, width = dims
    owners = n_list * n_slab
    depth = groups * width
    slots = owners * CAP
    l, y, s = lax.axis_index("list"), lax.axis_index("sub"), lax.axis_index("slab")
    me = l * n_slab + s

    def plane(i):
        dl, ds = i // n_slab, lax.rem(i, n_slab)
        pl_, ps = lax.rem(l + dl, n_list), lax.rem(s + ds, n_slab)
        return (pl_, y, ps), pl_ * n_slab + ps

    offs = [0]
    for d in range(1, n_sub // 2 + 1):
        offs += [d] if 2 * d == n_sub else [d, n_sub - d]

    cen_copy = pltpu.make_async_copy(cen_ref, cen_v, lsem.at[0])
    cb_copy = pltpu.make_async_copy(cb_ref, cb_v, lsem.at[1])
    self_copy = pltpu.make_async_copy(
        vec_ref.at[pl.ds(pl.multiple_of(y * depth, depth), depth)], ybuf.at[0], lsem.at[2]
    )
    self_copy.start()
    cb_copy.start()
    cen_copy.start()

    bar = pltpu.get_barrier_semaphore()
    for d in range(1, n_sub):
        pl.semaphore_signal(bar, 1, device_id=(l, lax.rem(y + d, n_sub), s), device_id_type=MESH)

    def greet(i, _):
        pl.semaphore_signal(bar, 1, device_id=plane(i)[0], device_id_type=MESH)
        return 0

    lax.fori_loop(1, owners, greet, 0)

    earlier = (iota((cols, cols), 0) < iota((cols, cols), 1)).astype(BF16)

    def place(idrow):
        owner = idrow // n_lists
        hit = (iota((owners, cols), 0) == owner)
        before = dot(hit.astype(BF16), earlier)
        rank = jnp.sum(jnp.where(hit, before, 0.0), axis=0, keepdims=True).astype(I32)
        return hit, rank, owner * CAP + rank

    def pack(r):
        slot = slotbuf[r]
        put = (iota((slots, cols), 0) == slot).astype(BF16)
        a, b, c = split3(ybuf[r])
        send[r] = dot(put, a, 1, 1) + dot(put, b, 1, 1) + dot(put, c, 1, 1)

    def send_round(r):
        def go(i, _):
            dev, j = plane(i)
            pltpu.make_async_remote_copy(
                src_ref=send.at[r, pl.ds(pl.multiple_of(j * CAP, CAP), CAP)],
                dst_ref=recv.at[r, pl.ds(pl.multiple_of(me * CAP, CAP), CAP)],
                send_sem=dsend.at[r], recv_sem=drecv.at[r], device_id=dev, device_id_type=MESH,
            ).start()
            return 0

        lax.fori_loop(1, owners, go, 0)
        mine = pl.ds(pl.multiple_of(me * CAP, CAP), CAP)
        pltpu.make_async_copy(send.at[r, mine], recv.at[r, mine], lsem.at[3 + r]).start()

    idbuf[0] = ids_ref[...]
    slotbuf[0] = place(idbuf[0])[2]
    self_copy.wait()
    pack(0)

    pl.semaphore_wait(bar, owners - 1 + n_sub - 1)

    for r in range(1, n_sub):
        d = n_sub - offs[r]
        yy = lax.rem(y + d, n_sub)
        pltpu.make_async_remote_copy(
            src_ref=idbuf.at[0], dst_ref=idbuf.at[r],
            send_sem=isend, recv_sem=irecv, device_id=(l, yy, s), device_id_type=MESH,
        ).start()
    for r in range(1, n_sub):
        d = n_sub - offs[r]
        yy = lax.rem(y + d, n_sub)
        pltpu.make_async_remote_copy(
            src_ref=vec_ref.at[pl.ds(pl.multiple_of(yy * depth, depth), depth)], dst_ref=ybuf.at[r],
            send_sem=ysend, recv_sem=yrecv.at[r], device_id=(l, yy, s), device_id_type=MESH,
        ).start()
    send_round(0)

    cb_copy.wait()
    log2e = math.log2(math.e)
    for g in range(groups):
        cbt = jnp.swapaxes(cb_v[g], 0, 1)
        for h in range(codes // 128):
            for q in range(width // 4):
                cbp[(g * (codes // 128) + h) * (width // 4) + q, 0:4] = cbt[q * 4:q * 4 + 4, h * 128:h * 128 + 128]
        scaled = cbt * (2.0 / SOFTMAX_HEAT * log2e)
        norm = jnp.sum(cbt * cbt, axis=0, keepdims=True) * (-log2e / SOFTMAX_HEAT)
        c1, c2, c3 = (v.astype(F32) for v in split3(scaled))
        n1, n2, n3 = (v.astype(F32) for v in split3(norm))
        row = iota((16, codes), 0)
        tail = jnp.where(row == 0, n1, jnp.where(row == 1, n2, jnp.where(row == 2, n3, 0.0)))
        stack = jnp.concatenate([c1, c2, c3, c1, c2, c1, tail, jnp.zeros((256 - 6 * width - 16, codes), F32)], axis=0)
        cbk[g] = jnp.swapaxes(stack, 0, 1).astype(BF16)
    acc[...] = jnp.zeros_like(acc)

    whole = idbuf.at[pl.ds(1, n_sub - 1)]
    pltpu.make_async_copy(whole, whole, irecv).wait()
    labels = jnp.zeros((owners, 128), F32)
    for r in range(n_sub):
        idrow = idbuf[r]
        hit, rank, slot = place(idrow)
        if r:
            slotbuf[r] = slot
        number = idrow - (idrow // n_lists) * n_lists + 1
        high, low = (number // 64).astype(F32), (number % 64).astype(F32)
        q = iota((128, cols), 0) - (r * CAP)
        value = jnp.where(q == rank, high, jnp.where(q == rank + 32, low, 0.0)).astype(BF16)
        labels = labels + dot(hit.astype(BF16), value, 1, 1)
    labsend[...] = labels.reshape(owners, 1, 128)

    def send_labels(i, _):
        dev, j = plane(i)
        pltpu.make_async_remote_copy(
            src_ref=labsend.at[j], dst_ref=labrecv.at[me],
            send_sem=labs, recv_sem=labr, device_id=dev, device_id_type=MESH,
        ).start()
        return 0

    lax.fori_loop(1, owners, send_labels, 0)
    labrecv[me] = labsend[me]

    for r in range(1, n_sub):
        pltpu.make_async_copy(ybuf.at[r], ybuf.at[r], yrecv.at[r]).wait()
        pack(r)
        send_round(r)

    most = labrecv.at[pl.ds(0, owners - 1)]
    pltpu.make_async_copy(most, most, labr).wait()
    lab = labrecv[...].reshape(owners, 128).astype(BF16)
    from_j = iota((owners, slots), 1) // CAP == iota((owners, slots), 0)
    for r in range(n_sub):
        want = iota((128, slots), 1) % CAP + r * CAP
        q = iota((128, slots), 0)
        pick = jnp.where(q == want, 64.0, jnp.where(q == want + 32, 1.0, 0.0)).astype(BF16)
        labrow[r] = jnp.sum(jnp.where(from_j, dot(lab, pick), 0.0), axis=0, keepdims=True)
    cen_copy.wait()
    chunk = 512

    def gather(r, _):
        number = labrow[r].astype(I32) - 1
        total = jnp.zeros((depth, slots), F32)
        for k in range(n_lists // chunk):
            hot = (iota((chunk, slots), 0) == number - k * chunk).astype(BF16)
            total = total + dot(cen_v[:, k * chunk:(k + 1) * chunk], hot)
        cent[r] = total
        return 0

    lax.fori_loop(0, n_sub, gather, 0)

    def work(r, _):
        arrived = recv.at[r, pl.ds(0, slots - CAP)]
        pltpu.make_async_copy(arrived, arrived, drecv.at[r]).wait()
        mine = pl.ds(pl.multiple_of(me * CAP, CAP), CAP)
        pltpu.make_async_copy(send.at[r, mine], recv.at[r, mine], lsem.at[3 + r]).wait()
        present = (labrow[r] > 0.5).astype(F32)
        residual = jnp.swapaxes(recv[r], 0, 1) - cent[r]
        row = iota((16, slots), 0)
        ones = jnp.where(row < 3, 1.0, 0.0).astype(BF16)
        fill = jnp.zeros((256 - 6 * width - 16, slots), BF16)
        for g in range(groups):
            part = residual[g * width:(g + 1) * width]
            r1, r2, r3 = split3(part)
            stack = jnp.concatenate([r1, r1, r1, r2, r2, r3, ones, fill], axis=0)
            logits = dot(cbk[g], stack)
            e = jnp.exp2(logits - jnp.max(logits, axis=0, keepdims=True))
            inv = present / jnp.sum(e, axis=0, keepdims=True)
            w = jnp.concatenate([part * inv, jnp.where(row == 0, inv, 0.0)], axis=0)
            w = jnp.concatenate(split3(w), axis=0)
            e1 = e.astype(BF16)
            e2 = (e - e1.astype(F32)).astype(BF16)
            acc[g] += dot(w, e1, 1, 1) + dot(w, e2, 1, 1)
        return 0

    lax.fori_loop(0, n_sub, work, 0)

    part_rows = width + 16
    for g in range(groups):
        t = acc[g]
        t = t[0:part_rows] + t[part_rows:2 * part_rows] + t[2 * part_rows:3 * part_rows]
        for h in range(codes // 128):
            for q in range(width // 4):
                p = (g * (codes // 128) + h) * (width // 4) + q
                arsend[p, 0:4] = t[q * 4:q * 4 + 4, h * 128:h * 128 + 128]
                arsend[p, 4:5] = t[width:width + 1, h * 128:h * 128 + 128]

    def scatter(i, _):
        dev, j = plane(i)
        pltpu.make_async_remote_copy(
            src_ref=arsend.at[j, pl.ds(0, 5)], dst_ref=arrecv.at[me, pl.ds(0, 5)],
            send_sem=rss, recv_sem=rsr, device_id=dev, device_id_type=MESH,
        ).start()
        return 0

    lax.fori_loop(1, owners, scatter, 0)
    arrecv[me, 0:5] = arsend[me, 0:5]
    some = arrecv.at[pl.ds(0, owners - 1), pl.ds(0, 5)]
    pltpu.make_async_copy(some, some, rsr).wait()
    total = jnp.sum(arrecv[:, 0:5], axis=0)
    finsend[...] = (total[0:4] + PRIOR_MASS * cbp[me, 0:4]) / (total[4:5] + PRIOR_MASS)

    def hand(i, _):
        dev, j = plane(i)
        pltpu.make_async_remote_copy(
            src_ref=finsend, dst_ref=finrecv.at[me],
            send_sem=ags, recv_sem=agr, device_id=dev, device_id_type=MESH,
        ).start()
        return 0

    lax.fori_loop(1, owners, hand, 0)
    finrecv[me] = finsend[...]

    pltpu.make_async_copy(whole, whole, isend).wait()
    others = ybuf.at[pl.ds(1, n_sub - 1)]
    pltpu.make_async_copy(others, others, ysend).wait()
    pltpu.make_async_copy(most, most, labs).wait()
    for r in range(n_sub):
        gone = send.at[r, pl.ds(0, slots - CAP)]
        pltpu.make_async_copy(gone, gone, dsend.at[r]).wait()
    pltpu.make_async_copy(some, some, rss).wait()

    last = finrecv.at[pl.ds(0, owners - 1)]
    pltpu.make_async_copy(last, last, agr).wait()
    for g in range(groups):
        for h in range(codes // 128):
            for q in range(width // 4):
                p = (g * (codes // 128) + h) * (width // 4) + q
                out_ref[g, q * 4:q * 4 + 4, h * 128:h * 128 + 128] = finrecv[p]
    pltpu.make_async_copy(last, last, ags).wait()


def per_device(vectors, centroids, codebook, list_ids):
    n_list, n_sub, n_slab = (lax.axis_size(a) for a in ("list", "sub", "slab"))
    owners = n_list * n_slab
    n_lists, cols = centroids.shape[1], vectors.shape[1]
    groups, codes, width = codebook.shape
    depth = groups * width
    slots = owners * CAP
    dims = (n_list, n_sub, n_slab, n_lists, cols, groups, codes, width)
    dma = pltpu.SemaphoreType.DMA
    hbm = pl.BlockSpec(memory_space=pl.ANY)
    vmem = pl.BlockSpec(memory_space=pltpu.VMEM)
    out = pl.pallas_call(
        functools.partial(kernel, dims),
        out_shape=jax.ShapeDtypeStruct((groups, width, codes), F32),
        in_specs=[vmem, hbm, hbm, hbm],
        out_specs=vmem,
        scratch_shapes=[
            pltpu.VMEM((depth, n_lists), BF16),
            pltpu.VMEM((groups, codes, width), F32),
            pltpu.VMEM((n_sub, depth, cols), F32),
            pltpu.VMEM((n_sub, 1, cols), I32),
            pltpu.VMEM((n_sub, 1, cols), I32),
            pltpu.VMEM((n_sub, slots, depth), F32),
            pltpu.VMEM((n_sub, slots, depth), F32),
            pltpu.VMEM((owners, 1, 128), F32),
            pltpu.VMEM((owners, 1, 128), F32),
            pltpu.VMEM((n_sub, 1, slots), F32),
            pltpu.VMEM((n_sub, depth, slots), F32),
            pltpu.VMEM((groups, codes, 256), BF16),
            pltpu.VMEM((owners, 8, 128), F32),
            pltpu.VMEM((groups, 3 * (width + 16), codes), F32),
            pltpu.VMEM((owners, 8, 128), F32),
            pltpu.VMEM((owners, 8, 128), F32),
            pltpu.VMEM((4, 128), F32),
            pltpu.VMEM((owners, 4, 128), F32),
            dma((3 + n_sub,)), dma, dma((n_sub,)), dma, dma, dma, dma, dma((n_sub,)), dma((n_sub,)),
            dma, dma, dma, dma,
        ],
        compiler_params=pltpu.CompilerParams(
            collective_id=0, has_side_effects=True, vmem_limit_bytes=48 << 20
        ),
    )(list_ids.reshape(1, cols), vectors, centroids, codebook)
    return jnp.swapaxes(out, 1, 2)


def solution(mesh):
    return jax.shard_map(
        per_device,
        mesh=mesh,
        in_specs=(
            P(None, ("list", "sub", "slab")),
            P("sub", ("list", "slab")),
            P("sub", None, None),
            P(("list", "sub", "slab")),
        ),
        out_specs=P("sub", None, None),
        check_vma=False,
    )
```

```python
import functools
import math

import jax
import jax.numpy as jnp
from jax import lax
from jax.experimental import pallas as pl
from jax.experimental.pallas import tpu as pltpu
from jax.sharding import PartitionSpec as P

SOFTMAX_HEAT = 8.0
PRIOR_MASS = 1.0
MESH = pl.DeviceIdType.MESH
F32, BF16, I32 = jnp.float32, jnp.bfloat16, jnp.int32
GROUPS = ((0,), (1,), (2, 3), (4, 5), (6, 7))
CAP = 4


def split3(x):
    a = x.astype(BF16)
    rest = x - a.astype(F32)
    b = rest.astype(BF16)
    c = (rest - b.astype(F32)).astype(BF16)
    return a, b, c


def dot(a, b, ca=1, cb=0):
    return lax.dot_general(a, b, (((ca,), (cb,)), ((), ())), preferred_element_type=F32)


def iota(shape, dim):
    return lax.broadcasted_iota(I32, shape, dim)


def kernel(
    dims,
    ids_ref, vec_ref, cen_ref, cb_ref,
    out_ref,
    cen_v, cb_v, ybuf, idbuf, ownbuf, rankbuf, send, recv, labsend, labrecv, labrow, cent, cbk, cbp, acc,
    arsend, arrecv, zsend, zrecv, finsend, finrecv,
    lsem, ysend, yrecv, isend, irecv, labs, labr, dsend, drecv, ars, arr,
):
    n_list, n_sub, n_slab, n_lists, cols, groups, codes, width = dims
    owners = n_list * n_slab
    depth = groups * width
    slots = owners * CAP
    l, y, s = lax.axis_index("list"), lax.axis_index("sub"), lax.axis_index("slab")
    me = l * n_slab + s

    cores, half = 2, n_list // 2
    far_first = sorted(range(n_slab), key=lambda d: -min(d, n_slab - d))
    slabs = [lax.rem(s + ds, n_slab) for ds in far_first]

    def wrap(v, n):
        return jnp.where(v >= n, v - n, v)

    def each_owner(do):
        def one_list(there, which):
            for w in which:
                do((there, y, slabs[w]), there * n_slab + slabs[w])

        one_list(wrap(l + half, n_list), range(n_slab))

        def two_lists(t, _):
            one_list(wrap(l + (half - t), n_list), range(n_slab))
            one_list(wrap(l + (half + t), n_list), range(n_slab))
            return 0

        lax.fori_loop(1, half, two_lists, 0)
        one_list(l, [w for w in range(n_slab) if far_first[w]])

    offs = [0]
    for d in range(1, n_sub // 2 + 1):
        offs += [d] if 2 * d == n_sub else [d, n_sub - d]

    parts = GROUPS if n_sub == 8 else tuple((r,) for r in range(n_sub))

    cen_copy = pltpu.make_async_copy(cen_ref, cen_v, lsem.at[0])
    cb_copy = pltpu.make_async_copy(cb_ref, cb_v, lsem.at[1])
    self_copy = pltpu.make_async_copy(
        vec_ref.at[pl.ds(pl.multiple_of(y * depth, depth), depth)], ybuf.at[0], lsem.at[2]
    )
    ids_copy = pltpu.make_async_copy(ids_ref, idbuf.at[0], lsem.at[3 + n_sub])
    ids_copy.start()
    self_copy.start()
    cb_copy.start()
    cen_copy.start()

    bar = pltpu.get_barrier_semaphore()
    each_owner(lambda dev, j: pl.semaphore_signal(bar, 1, device_id=dev, device_id_type=MESH))
    for d in range(1, n_sub):
        pl.semaphore_signal(bar, 1, device_id=(l, lax.rem(y + d, n_sub), s), device_id_type=MESH)


    earlier = (iota((cols, cols), 0) < iota((cols, cols), 1)).astype(BF16)

    def place(r):
        idrow = idbuf[r]
        owner = idrow // n_lists
        hit = (iota((owners, cols), 0) == owner)
        before = dot(hit.astype(BF16), earlier)
        rank = jnp.sum(jnp.where(hit, before, 0.0), axis=0, keepdims=True).astype(I32)
        number = idrow - owner * n_lists + 1
        return hit, rank, owner, number

    def rows_of(p):
        return parts[p][0] * slots, len(parts[p]) * slots

    def pack(p):
        base, count = rows_of(p)
        each = len(parts[p]) * CAP
        row = iota((count, cols), 0)
        total = None
        for i, r in enumerate(parts[p]):
            put = (row == ownbuf[r] * each + rankbuf[r] + i * CAP).astype(BF16)
            for v in split3(ybuf[r]):
                term = dot(put, v, 1, 1)
                total = term if total is None else total + term
        send[base:base + count] = total

    def send_part(p):
        base, count = rows_of(p)
        each = len(parts[p]) * CAP

        def go(dev, j):
            pltpu.make_async_remote_copy(
                src_ref=send.at[pl.ds(pl.multiple_of(base + j * each, CAP), each)],
                dst_ref=recv.at[pl.ds(pl.multiple_of(base + me * each, CAP), each)],
                send_sem=dsend.at[p], recv_sem=drecv.at[p], device_id=dev, device_id_type=MESH,
            ).start()

        each_owner(go)
        own_part(p).start()

    def own_part(p):
        base, _ = rows_of(p)
        each = len(parts[p]) * CAP
        mine = pl.ds(pl.multiple_of(base + me * each, CAP), each)
        return pltpu.make_async_copy(send.at[mine], recv.at[mine], lsem.at[3 + p])

    ids_copy.wait()
    _, rankbuf[0], ownbuf[0], _ = place(0)
    self_copy.wait()
    pack(0)

    pl.semaphore_wait(bar, owners - 1 + n_sub - 1)

    for r in range(1, n_sub):
        d = n_sub - offs[r]
        yy = lax.rem(y + d, n_sub)
        pltpu.make_async_remote_copy(
            src_ref=idbuf.at[0], dst_ref=idbuf.at[r],
            send_sem=isend, recv_sem=irecv, device_id=(l, yy, s), device_id_type=MESH,
        ).start()
    for r in range(1, n_sub):
        d = n_sub - offs[r]
        yy = lax.rem(y + d, n_sub)
        pltpu.make_async_remote_copy(
            src_ref=vec_ref.at[pl.ds(pl.multiple_of(yy * depth, depth), depth)], dst_ref=ybuf.at[r],
            send_sem=ysend, recv_sem=yrecv.at[r], device_id=(l, yy, s), device_id_type=MESH,
        ).start()
    send_part(0)

    whole = idbuf.at[pl.ds(1, n_sub - 1)]
    pltpu.make_async_copy(whole, whole, irecv).wait()
    labels = jnp.zeros((owners, 128), F32)
    for r in range(n_sub):
        hit, rank, owner, number = place(r)
        if r:
            rankbuf[r], ownbuf[r] = rank, owner
        high, low = (number // 64).astype(F32), (number % 64).astype(F32)
        q = iota((128, cols), 0) - (r * CAP)
        value = jnp.where(q == rank, high, jnp.where(q == rank + 32, low, 0.0)).astype(BF16)
        labels = labels + dot(hit.astype(BF16), value, 1, 1)
    labsend[...] = labels.reshape(owners, 1, 128)
    labrecv[me] = labsend[me]

    def send_labels(dev, j):
        pltpu.make_async_remote_copy(
            src_ref=labsend.at[j], dst_ref=labrecv.at[me],
            send_sem=labs, recv_sem=labr, device_id=dev, device_id_type=MESH,
        ).start()

    for p in range(1, len(parts)):
        for r in parts[p]:
            pltpu.make_async_copy(ybuf.at[r], ybuf.at[r], yrecv.at[r]).wait()
        pack(p)
        send_part(p)
        if p == 1:
            each_owner(send_labels)

    cb_copy.wait()
    log2e = math.log2(math.e)
    for g in range(groups):
        cbt = cb_v[g]
        for h in range(codes // 128):
            cbp[g * (codes // 128) + h] = cbt[:, h * 128:h * 128 + 128]
        scaled = cbt * (2.0 / SOFTMAX_HEAT * log2e)
        norm = jnp.sum(cbt * cbt, axis=0, keepdims=True) * (-log2e / SOFTMAX_HEAT)
        c1, c2, c3 = (v.astype(F32) for v in split3(scaled))
        n1, n2, n3 = (v.astype(F32) for v in split3(norm))
        row = iota((16, codes), 0)
        tail = jnp.where(row == 0, n1, jnp.where(row == 1, n2, jnp.where(row == 2, n3, 0.0)))
        stack = jnp.concatenate([c1, c2, c3, c1, c2, c1, tail, jnp.zeros((256 - 6 * width - 16, codes), F32)], axis=0)
        cbk[g] = jnp.swapaxes(stack, 0, 1).astype(BF16)
    acc[...] = jnp.zeros_like(acc)

    most = labrecv.at[pl.ds(0, owners - 1)]
    pltpu.make_async_copy(most, most, labr).wait()
    lab = labrecv[...].reshape(owners, 128).astype(BF16)
    for p, members in enumerate(parts):
        each = len(members) * CAP
        for b in range(len(members)):
            lane = iota((128, slots), 1) + b * slots
            want = lane % each + members[0] * CAP
            q = iota((128, slots), 0)
            pick = jnp.where(q == want, 64.0, jnp.where(q == want + 32, 1.0, 0.0)).astype(BF16)
            from_j = (iota((owners, slots), 1) + b * slots) // each == iota((owners, slots), 0)
            labrow[members[b]] = jnp.sum(jnp.where(from_j, dot(lab, pick), 0.0), axis=0, keepdims=True)
    cen_copy.wait()
    chunk = 512

    def gather(r, _):
        number = labrow[r].astype(I32) - 1
        total = jnp.zeros((depth, slots), F32)
        for k in range(n_lists // chunk):
            hot = (iota((chunk, slots), 0) == number - k * chunk).astype(BF16)
            total = total + dot(cen_v[:, k * chunk:(k + 1) * chunk], hot)
        cent[r] = total
        return 0

    lax.fori_loop(0, n_sub, gather, 0)

    def work(r, _):
        present = (labrow[r] > 0.5).astype(F32)
        residual = jnp.swapaxes(recv[pl.ds(pl.multiple_of(r * slots, slots), slots)], 0, 1) - cent[r]
        row = iota((16, slots), 0)
        ones = jnp.where(row < 3, 1.0, 0.0).astype(BF16)
        fill = jnp.zeros((256 - 6 * width - 16, slots), BF16)
        for g in range(groups):
            part = residual[g * width:(g + 1) * width]
            r1, r2, r3 = split3(part)
            stack = jnp.concatenate([r1, r1, r1, r2, r2, r3, ones, fill], axis=0)
            logits = dot(cbk[g], stack)
            e = jnp.exp2(logits - jnp.max(logits, axis=0, keepdims=True))
            inv = present / jnp.sum(e, axis=0, keepdims=True)
            w = jnp.concatenate([part * inv, jnp.where(row == 0, inv, 0.0)], axis=0)
            w = jnp.concatenate(split3(w), axis=0)
            e1 = e.astype(BF16)
            e2 = (e - e1.astype(F32)).astype(BF16)
            acc[g] += dot(w, e1, 1, 1) + dot(w, e2, 1, 1)
        return 0

    for p, members in enumerate(parts):
        base, count = rows_of(p)
        arrived = recv.at[pl.ds(base, count - len(members) * CAP)]
        pltpu.make_async_copy(arrived, arrived, drecv.at[p]).wait()
        own_part(p).wait()
        if len(members) == 1:
            work(members[0], 0)
        else:
            lax.fori_loop(members[0], members[-1] + 1, work, 0)

    z, core = l // cores, lax.rem(l, cores)
    n_z, n_k = n_list // cores, n_slab * cores
    k = s * cores + core
    part_rows = width + 16
    for g in range(groups):
        t = acc[g]
        t = t[0:width + 8] + t[part_rows:part_rows + width + 8] + t[2 * part_rows:2 * part_rows + width + 8]
        for h in range(codes // 128):
            arsend[g * (codes // 128) + h] = t[:, h * 128:h * 128 + 128]

    def along_k(i):
        to_s = lax.rem(s + i // cores, n_slab)
        to_c = lax.rem(core + i, cores)
        return (z * cores + to_c, y, to_s), to_s * cores + to_c

    order_k = sorted(range(1, n_k), key=lambda i: -min(i // cores, n_slab - i // cores))
    order_z = sorted(range(1, n_z), key=lambda i: -min(i, n_z - i))
    rows = width + 1
    for i in order_k:
        dev, j = along_k(i)
        pltpu.make_async_remote_copy(
            src_ref=arsend.at[j, pl.ds(0, rows)], dst_ref=arrecv.at[k, pl.ds(0, rows)],
            send_sem=ars.at[0], recv_sem=arr.at[0], device_id=dev, device_id_type=MESH,
        ).start()
    arrecv[k] = arsend[k]
    got_k = arrecv.at[pl.ds(0, n_k - 1), pl.ds(0, rows)]
    pltpu.make_async_copy(got_k, got_k, arr.at[0]).wait()
    zsend[...] = jnp.sum(arrecv[...], axis=0)
    for i in order_z:
        pltpu.make_async_remote_copy(
            src_ref=zsend.at[pl.ds(0, rows)], dst_ref=zrecv.at[z, pl.ds(0, rows)],
            send_sem=ars.at[1], recv_sem=arr.at[1],
            device_id=(lax.rem(z + i, n_z) * cores + core, y, s), device_id_type=MESH,
        ).start()
    zrecv[z] = zsend[...]
    got_z = zrecv.at[pl.ds(0, n_z - 1), pl.ds(0, rows)]
    pltpu.make_async_copy(got_z, got_z, arr.at[1]).wait()
    total = jnp.sum(zrecv[...], axis=0)
    finsend[...] = (total[0:width] + PRIOR_MASS * cbp[k]) / (total[width:width + 1] + PRIOR_MASS)
    for i in order_k:
        dev, j = along_k(i)
        pltpu.make_async_remote_copy(
            src_ref=finsend, dst_ref=finrecv.at[k],
            send_sem=ars.at[2], recv_sem=arr.at[2], device_id=dev, device_id_type=MESH,
        ).start()
    finrecv[k] = finsend[...]

    pltpu.make_async_copy(whole, whole, isend).wait()
    others = ybuf.at[pl.ds(1, n_sub - 1)]
    pltpu.make_async_copy(others, others, ysend).wait()
    pltpu.make_async_copy(most, most, labs).wait()
    for p, members in enumerate(parts):
        base, count = rows_of(p)
        gone = send.at[pl.ds(base, count - len(members) * CAP)]
        pltpu.make_async_copy(gone, gone, dsend.at[p]).wait()
    pltpu.make_async_copy(got_k, got_k, ars.at[0]).wait()
    pltpu.make_async_copy(got_z, got_z, ars.at[1]).wait()

    last = finrecv.at[pl.ds(0, n_k - 1)]
    pltpu.make_async_copy(last, last, arr.at[2]).wait()
    for g in range(groups):
        for h in range(codes // 128):
            out_ref[g, :, h * 128:h * 128 + 128] = finrecv[g * (codes // 128) + h]
    pltpu.make_async_copy(last, last, ars.at[2]).wait()


def per_device(vectors, centroids, codebook, list_ids):
    n_list, n_sub, n_slab = (lax.axis_size(a) for a in ("list", "sub", "slab"))
    owners = n_list * n_slab
    n_lists, cols = centroids.shape[1], vectors.shape[1]
    groups, codes, width = codebook.shape
    depth = groups * width
    slots = owners * CAP
    n_z, n_k = n_list // 2, n_slab * 2
    dims = (n_list, n_sub, n_slab, n_lists, cols, groups, codes, width)
    dma = pltpu.SemaphoreType.DMA
    hbm = pl.BlockSpec(memory_space=pl.ANY)
    vmem = pl.BlockSpec(memory_space=pltpu.VMEM)
    out = pl.pallas_call(
        functools.partial(kernel, dims),
        out_shape=jax.ShapeDtypeStruct((groups, width, codes), F32),
        in_specs=[hbm, hbm, hbm, hbm],
        out_specs=vmem,
        scratch_shapes=[
            pltpu.VMEM((depth, n_lists), BF16),
            pltpu.VMEM((groups, width, codes), F32),
            pltpu.VMEM((n_sub, depth, cols), F32),
            pltpu.VMEM((n_sub, 1, cols), I32),
            pltpu.VMEM((n_sub, 1, cols), I32),
            pltpu.VMEM((n_sub, 1, cols), I32),
            pltpu.VMEM((n_sub * slots, depth), F32),
            pltpu.VMEM((n_sub * slots, depth), F32),
            pltpu.VMEM((owners, 1, 128), F32),
            pltpu.VMEM((owners, 1, 128), F32),
            pltpu.VMEM((n_sub, 1, slots), F32),
            pltpu.VMEM((n_sub, depth, slots), F32),
            pltpu.VMEM((groups, codes, 256), BF16),
            pltpu.VMEM((n_k, width, 128), F32),
            pltpu.VMEM((groups, 3 * (width + 16), codes), F32),
            pltpu.VMEM((n_k, width + 8, 128), F32),
            pltpu.VMEM((n_k, width + 8, 128), F32),
            pltpu.VMEM((width + 8, 128), F32),
            pltpu.VMEM((n_z, width + 8, 128), F32),
            pltpu.VMEM((width, 128), F32),
            pltpu.VMEM((n_k, width, 128), F32),
            dma((4 + n_sub,)), dma, dma((n_sub,)), dma, dma, dma, dma, dma((n_sub,)), dma((n_sub,)),
            dma((3,)), dma((3,)),
        ],
        compiler_params=pltpu.CompilerParams(
            collective_id=0, has_side_effects=True, vmem_limit_bytes=60 << 20
        ),
    )(list_ids.reshape(1, cols), vectors, centroids, jnp.swapaxes(codebook, 1, 2))
    return jnp.swapaxes(out, 1, 2)


def solution(mesh):
    return jax.shard_map(
        per_device,
        mesh=mesh,
        in_specs=(
            P(None, ("list", "sub", "slab")),
            P("sub", ("list", "slab")),
            P("sub", None, None),
            P(("list", "sub", "slab")),
        ),
        out_specs=P("sub", None, None),
        check_vma=False,
    )
```

```python
import functools
import math

import jax
import jax.numpy as jnp
from jax import lax
from jax.experimental import pallas as pl
from jax.experimental.pallas import tpu as pltpu
from jax.sharding import PartitionSpec as P

SOFTMAX_HEAT = 8.0
PRIOR_MASS = 1.0
MESH = pl.DeviceIdType.MESH
F32, BF16, I32 = jnp.float32, jnp.bfloat16, jnp.int32
GROUPS = ((0,), (1,), (2,), (3, 4), (5, 6), (7,))
CAP = 4


def split3(x):
    a = x.astype(BF16)
    rest = x - a.astype(F32)
    b = rest.astype(BF16)
    c = (rest - b.astype(F32)).astype(BF16)
    return a, b, c


def dot(a, b, ca=1, cb=0):
    return lax.dot_general(a, b, (((ca,), (cb,)), ((), ())), preferred_element_type=F32)


def iota(shape, dim):
    return lax.broadcasted_iota(I32, shape, dim)


def kernel(
    dims,
    ids_ref, vec_ref, cen_ref, cb_ref,
    out_ref,
    cen_v, cb_v, ybuf, idbuf, ownbuf, rankbuf, send, recv, labsend, labrecv, labrow, cent, cbk, cbp, acc,
    arsend, arrecv, zsend, zrecv, finsend, finrecv,
    lsem, ysend, yrecv, isend, irecv, labs, labr, dsend, drecv, ars, arr,
):
    n_list, n_sub, n_slab, n_lists, cols, groups, codes, width = dims
    owners = n_list * n_slab
    depth = groups * width
    slots = owners * CAP
    l, y, s = lax.axis_index("list"), lax.axis_index("sub"), lax.axis_index("slab")
    me = l * n_slab + s

    cores, half = 2, n_list // 2
    far_first = sorted(range(n_slab), key=lambda d: -min(d, n_slab - d))
    slabs = [lax.rem(s + ds, n_slab) for ds in far_first]

    def wrap(v, n):
        return jnp.where(v >= n, v - n, v)

    def each_owner(do):
        def one_list(there, which):
            for w in which:
                do((there, y, slabs[w]), there * n_slab + slabs[w])

        one_list(wrap(l + half, n_list), range(n_slab))

        def two_lists(t, _):
            one_list(wrap(l + (half - t), n_list), range(n_slab))
            one_list(wrap(l + (half + t), n_list), range(n_slab))
            return 0

        lax.fori_loop(1, half, two_lists, 0)
        one_list(l, [w for w in range(n_slab) if far_first[w]])

    offs = [0]
    for d in range(1, n_sub // 2 + 1):
        offs += [d] if 2 * d == n_sub else [d, n_sub - d]

    parts = GROUPS if n_sub == 8 else tuple((r,) for r in range(n_sub))

    cen_copy = pltpu.make_async_copy(cen_ref, cen_v, lsem.at[0])
    cb_copy = pltpu.make_async_copy(cb_ref, cb_v, lsem.at[1])
    self_copy = pltpu.make_async_copy(
        vec_ref.at[pl.ds(pl.multiple_of(y * depth, depth), depth)], ybuf.at[0], lsem.at[2]
    )
    ids_copy = pltpu.make_async_copy(ids_ref, idbuf.at[0], lsem.at[3 + n_sub])
    ids_copy.start()
    self_copy.start()
    cb_copy.start()
    cen_copy.start()

    bar = pltpu.get_barrier_semaphore()
    each_owner(lambda dev, j: pl.semaphore_signal(bar, 1, device_id=dev, device_id_type=MESH))
    for d in range(1, n_sub):
        pl.semaphore_signal(bar, 1, device_id=(l, lax.rem(y + d, n_sub), s), device_id_type=MESH)


    earlier = (iota((cols, cols), 0) < iota((cols, cols), 1)).astype(BF16)

    def place(r):
        idrow = idbuf[r]
        owner = idrow // n_lists
        hit = (iota((owners, cols), 0) == owner)
        before = dot(hit.astype(BF16), earlier)
        rank = jnp.sum(jnp.where(hit, before, 0.0), axis=0, keepdims=True).astype(I32)
        number = idrow - owner * n_lists + 1
        return hit, rank, owner, number

    def rows_of(p):
        return parts[p][0] * slots, len(parts[p]) * slots

    def pack(p):
        base, count = rows_of(p)
        each = len(parts[p]) * CAP
        row = iota((count, cols), 0)
        total = None
        for i, r in enumerate(parts[p]):
            put = (row == ownbuf[r] * each + rankbuf[r] + i * CAP).astype(BF16)
            for v in split3(ybuf[r]):
                term = dot(put, v, 1, 1)
                total = term if total is None else total + term
        send[base:base + count] = total

    def send_part(p):
        base, count = rows_of(p)
        each = len(parts[p]) * CAP

        def go(dev, j):
            pltpu.make_async_remote_copy(
                src_ref=send.at[pl.ds(pl.multiple_of(base + j * each, CAP), each)],
                dst_ref=recv.at[pl.ds(pl.multiple_of(base + me * each, CAP), each)],
                send_sem=dsend.at[p], recv_sem=drecv.at[p], device_id=dev, device_id_type=MESH,
            ).start()

        each_owner(go)
        own_part(p).start()

    def own_part(p):
        base, _ = rows_of(p)
        each = len(parts[p]) * CAP
        mine = pl.ds(pl.multiple_of(base + me * each, CAP), each)
        return pltpu.make_async_copy(send.at[mine], recv.at[mine], lsem.at[3 + p])

    ids_copy.wait()
    _, rankbuf[0], ownbuf[0], _ = place(0)
    self_copy.wait()
    pack(0)

    pl.semaphore_wait(bar, owners - 1 + n_sub - 1)

    for r in range(1, n_sub):
        d = n_sub - offs[r]
        yy = lax.rem(y + d, n_sub)
        pltpu.make_async_remote_copy(
            src_ref=idbuf.at[0], dst_ref=idbuf.at[r],
            send_sem=isend, recv_sem=irecv, device_id=(l, yy, s), device_id_type=MESH,
        ).start()
    for r in range(1, n_sub):
        d = n_sub - offs[r]
        yy = lax.rem(y + d, n_sub)
        pltpu.make_async_remote_copy(
            src_ref=vec_ref.at[pl.ds(pl.multiple_of(yy * depth, depth), depth)], dst_ref=ybuf.at[r],
            send_sem=ysend, recv_sem=yrecv.at[r], device_id=(l, yy, s), device_id_type=MESH,
        ).start()
    send_part(0)

    whole = idbuf.at[pl.ds(1, n_sub - 1)]
    pltpu.make_async_copy(whole, whole, irecv).wait()
    labels = jnp.zeros((owners, 128), F32)
    for r in range(n_sub):
        hit, rank, owner, number = place(r)
        if r:
            rankbuf[r], ownbuf[r] = rank, owner
        high, low = (number // 64).astype(F32), (number % 64).astype(F32)
        q = iota((128, cols), 0) - (r * CAP)
        value = jnp.where(q == rank, high, jnp.where(q == rank + 32, low, 0.0)).astype(BF16)
        labels = labels + dot(hit.astype(BF16), value, 1, 1)
    labsend[...] = labels.reshape(owners, 1, 128)
    labrecv[me] = labsend[me]

    def send_labels(dev, j):
        pltpu.make_async_remote_copy(
            src_ref=labsend.at[j], dst_ref=labrecv.at[me],
            send_sem=labs, recv_sem=labr, device_id=dev, device_id_type=MESH,
        ).start()

    for p in range(1, len(parts)):
        for r in parts[p]:
            pltpu.make_async_copy(ybuf.at[r], ybuf.at[r], yrecv.at[r]).wait()
        pack(p)
        send_part(p)
        if p == 1:
            each_owner(send_labels)

    cb_copy.wait()
    log2e = math.log2(math.e)
    for g in range(groups):
        cbt = cb_v[g]
        for h in range(codes // 128):
            cbp[g * (codes // 128) + h] = cbt[:, h * 128:h * 128 + 128]
        scaled = cbt * (2.0 / SOFTMAX_HEAT * log2e)
        norm = jnp.sum(cbt * cbt, axis=0, keepdims=True) * (-log2e / SOFTMAX_HEAT)
        c1, c2, c3 = (v.astype(F32) for v in split3(scaled))
        n1, n2, n3 = (v.astype(F32) for v in split3(norm))
        row = iota((16, codes), 0)
        tail = jnp.where(row == 0, n1, jnp.where(row == 1, n2, jnp.where(row == 2, n3, 0.0)))
        stack = jnp.concatenate([c1, c2, c3, c1, c2, c1, tail, jnp.zeros((256 - 6 * width - 16, codes), F32)], axis=0)
        cbk[g] = jnp.swapaxes(stack, 0, 1).astype(BF16)
    acc[...] = jnp.zeros_like(acc)

    most = labrecv.at[pl.ds(0, owners - 1)]
    pltpu.make_async_copy(most, most, labr).wait()
    lab = labrecv[...].reshape(owners, 128).astype(BF16)
    for p, members in enumerate(parts):
        each = len(members) * CAP
        for b in range(len(members)):
            lane = iota((128, slots), 1) + b * slots
            want = lane % each + members[0] * CAP
            q = iota((128, slots), 0)
            pick = jnp.where(q == want, 64.0, jnp.where(q == want + 32, 1.0, 0.0)).astype(BF16)
            from_j = (iota((owners, slots), 1) + b * slots) // each == iota((owners, slots), 0)
            labrow[members[b]] = jnp.sum(jnp.where(from_j, dot(lab, pick), 0.0), axis=0, keepdims=True)
    cen_copy.wait()
    chunk = 512

    def gather(r, _):
        number = labrow[r].astype(I32) - 1
        total = jnp.zeros((depth, slots), F32)
        for k in range(n_lists // chunk):
            hot = (iota((chunk, slots), 0) == number - k * chunk).astype(BF16)
            total = total + dot(cen_v[:, k * chunk:(k + 1) * chunk], hot)
        cent[r] = total
        return 0

    lax.fori_loop(0, n_sub, gather, 0)

    row = iota((16, slots), 0)

    def prepare(r):
        present = (labrow[r] > 0.5).astype(F32)
        arrived = recv[pl.ds(pl.multiple_of(r * slots, slots), slots)]
        return present, jnp.swapaxes(arrived, 0, 1) - cent[r]

    def sums(g, present, residual):
        part = residual[g * width:(g + 1) * width]
        r1, r2, r3 = split3(part)
        ones = jnp.where(row < 3, 1.0, 0.0).astype(BF16)
        fill = jnp.zeros((256 - 6 * width - 16, slots), BF16)
        stack = jnp.concatenate([r1, r1, r1, r2, r2, r3, ones, fill], axis=0)
        logits = dot(cbk[g], stack)
        e = jnp.exp2(logits - jnp.max(logits, axis=0, keepdims=True))
        inv = present / jnp.sum(e, axis=0, keepdims=True)
        w = jnp.concatenate([part * inv, jnp.where(row == 0, inv, 0.0)], axis=0)
        w = jnp.concatenate(split3(w), axis=0)
        e1 = e.astype(BF16)
        e2 = (e - e1.astype(F32)).astype(BF16)
        return dot(w, e1, 1, 1) + dot(w, e2, 1, 1)

    def work(r, _):
        present, residual = prepare(r)
        for g in range(groups):
            acc[g] += sums(g, present, residual)
        return 0

    def arrival(p):
        base, count = rows_of(p)
        arrived = recv.at[pl.ds(base, count - len(parts[p]) * CAP)]
        pltpu.make_async_copy(arrived, arrived, drecv.at[p]).wait()
        own_part(p).wait()

    for p, members in enumerate(parts[:-1]):
        arrival(p)
        if len(members) == 1:
            work(members[0], 0)
        else:
            lax.fori_loop(members[0], members[-1] + 1, work, 0)

    z, core = l // cores, lax.rem(l, cores)
    n_z, n_k = n_list // cores, n_slab * cores
    k = s * cores + core
    rows, blocks = width + 1, codes // 128

    def along_k(i):
        to_s = lax.rem(s + i // cores, n_slab)
        to_c = lax.rem(core + i, cores)
        return (z * cores + to_c, y, to_s), to_s * cores + to_c

    order_k = sorted(range(1, n_k), key=lambda i: -min(i // cores, n_slab - i // cores))
    order_z = sorted(range(1, n_z), key=lambda i: -min(i, n_z - i))

    def give(j):
        pltpu.make_async_remote_copy(
            src_ref=arsend.at[j, pl.ds(0, rows)], dst_ref=arrecv.at[k, pl.ds(0, rows)],
            send_sem=ars.at[0], recv_sem=arr.at[0],
            device_id=(z * cores + j % cores, y, j // cores), device_id_type=MESH,
        ).start()

    for p in range(len(parts) - 1, len(parts)):
        arrival(p)
        for r in parts[p][:-1]:
            work(r, 0)
        present, residual = prepare(parts[p][-1])
        for g in range(groups):
            t = acc[g] + sums(g, present, residual)
            t = sum(t[i * (width + 16):i * (width + 16) + width + 8] for i in range(3))
            for h in range(blocks):
                j = g * blocks + h
                arsend[j] = t[:, h * 128:h * 128 + 128]
                pl.when(k != j)(functools.partial(give, j))
    arrecv[k] = arsend[k]
    got_k = arrecv.at[pl.ds(0, n_k - 1), pl.ds(0, rows)]
    pltpu.make_async_copy(got_k, got_k, arr.at[0]).wait()
    zsend[...] = jnp.sum(arrecv[...], axis=0)
    for i in order_z:
        pltpu.make_async_remote_copy(
            src_ref=zsend.at[pl.ds(0, rows)], dst_ref=zrecv.at[z, pl.ds(0, rows)],
            send_sem=ars.at[1], recv_sem=arr.at[1],
            device_id=(lax.rem(z + i, n_z) * cores + core, y, s), device_id_type=MESH,
        ).start()
    zrecv[z] = zsend[...]
    got_z = zrecv.at[pl.ds(0, n_z - 1), pl.ds(0, rows)]
    pltpu.make_async_copy(got_z, got_z, arr.at[1]).wait()
    total = jnp.sum(zrecv[...], axis=0)
    finsend[...] = (total[0:width] + PRIOR_MASS * cbp[k]) / (total[width:width + 1] + PRIOR_MASS)
    for i in order_k:
        dev, j = along_k(i)
        pltpu.make_async_remote_copy(
            src_ref=finsend, dst_ref=finrecv.at[k],
            send_sem=ars.at[2], recv_sem=arr.at[2], device_id=dev, device_id_type=MESH,
        ).start()
    finrecv[k] = finsend[...]

    pltpu.make_async_copy(whole, whole, isend).wait()
    others = ybuf.at[pl.ds(1, n_sub - 1)]
    pltpu.make_async_copy(others, others, ysend).wait()
    pltpu.make_async_copy(most, most, labs).wait()
    for p, members in enumerate(parts):
        base, count = rows_of(p)
        gone = send.at[pl.ds(base, count - len(members) * CAP)]
        pltpu.make_async_copy(gone, gone, dsend.at[p]).wait()
    pltpu.make_async_copy(got_k, got_k, ars.at[0]).wait()
    pltpu.make_async_copy(got_z, got_z, ars.at[1]).wait()

    last = finrecv.at[pl.ds(0, n_k - 1)]
    pltpu.make_async_copy(last, last, arr.at[2]).wait()
    for g in range(groups):
        for h in range(codes // 128):
            out_ref[g, :, h * 128:h * 128 + 128] = finrecv[g * (codes // 128) + h]
    pltpu.make_async_copy(last, last, ars.at[2]).wait()


def per_device(vectors, centroids, codebook, list_ids):
    n_list, n_sub, n_slab = (lax.axis_size(a) for a in ("list", "sub", "slab"))
    owners = n_list * n_slab
    n_lists, cols = centroids.shape[1], vectors.shape[1]
    groups, codes, width = codebook.shape
    depth = groups * width
    slots = owners * CAP
    n_z, n_k = n_list // 2, n_slab * 2
    dims = (n_list, n_sub, n_slab, n_lists, cols, groups, codes, width)
    dma = pltpu.SemaphoreType.DMA
    hbm = pl.BlockSpec(memory_space=pl.ANY)
    vmem = pl.BlockSpec(memory_space=pltpu.VMEM)
    out = pl.pallas_call(
        functools.partial(kernel, dims),
        out_shape=pltpu.VMEM((groups, width, codes), F32),
        in_specs=[hbm, hbm, hbm, hbm],
        out_specs=vmem,
        scratch_shapes=[
            pltpu.VMEM((depth, n_lists), BF16),
            pltpu.VMEM((groups, width, codes), F32),
            pltpu.VMEM((n_sub, depth, cols), F32),
            pltpu.VMEM((n_sub, 1, cols), I32),
            pltpu.VMEM((n_sub, 1, cols), I32),
            pltpu.VMEM((n_sub, 1, cols), I32),
            pltpu.VMEM((n_sub * slots, depth), F32),
            pltpu.VMEM((n_sub * slots, depth), F32),
            pltpu.VMEM((owners, 1, 128), F32),
            pltpu.VMEM((owners, 1, 128), F32),
            pltpu.VMEM((n_sub, 1, slots), F32),
            pltpu.VMEM((n_sub, depth, slots), F32),
            pltpu.VMEM((groups, codes, 256), BF16),
            pltpu.VMEM((n_k, width, 128), F32),
            pltpu.VMEM((groups, 3 * (width + 16), codes), F32),
            pltpu.VMEM((n_k, width + 8, 128), F32),
            pltpu.VMEM((n_k, width + 8, 128), F32),
            pltpu.VMEM((width + 8, 128), F32),
            pltpu.VMEM((n_z, width + 8, 128), F32),
            pltpu.VMEM((width, 128), F32),
            pltpu.VMEM((n_k, width, 128), F32),
            dma((4 + n_sub,)), dma, dma((n_sub,)), dma, dma, dma, dma, dma((n_sub,)), dma((n_sub,)),
            dma((3,)), dma((3,)),
        ],
        compiler_params=pltpu.CompilerParams(
            collective_id=0, has_side_effects=True, vmem_limit_bytes=60 << 20
        ),
    )(list_ids.reshape(1, cols), vectors, centroids, jnp.swapaxes(codebook, 1, 2))
    return jnp.swapaxes(out, 1, 2)


def solution(mesh):
    return jax.shard_map(
        per_device,
        mesh=mesh,
        in_specs=(
            P(None, ("list", "sub", "slab")),
            P("sub", ("list", "slab")),
            P("sub", None, None),
            P(("list", "sub", "slab")),
        ),
        out_specs=P("sub", None, None),
        check_vma=False,
    )
```

```python
import functools
import math

import jax
import jax.numpy as jnp
from jax import lax
from jax.experimental import pallas as pl
from jax.experimental.pallas import tpu as pltpu
from jax.sharding import PartitionSpec as P

SOFTMAX_HEAT = 8.0
PRIOR_MASS = 1.0
MESH = pl.DeviceIdType.MESH
F32, BF16, I32 = jnp.float32, jnp.bfloat16, jnp.int32
GROUPS = ((0,), (1,), (2,), (3, 4), (5, 6), (7,))
CAP = 4


def split3(x):
    a = x.astype(BF16)
    rest = x - a.astype(F32)
    b = rest.astype(BF16)
    c = (rest - b.astype(F32)).astype(BF16)
    return a, b, c


def dot(a, b, ca=1, cb=0):
    return lax.dot_general(a, b, (((ca,), (cb,)), ((), ())), preferred_element_type=F32)


def iota(shape, dim):
    return lax.broadcasted_iota(I32, shape, dim)


def kernel(
    dims,
    ids_ref, vec_ref, cen_ref, cb_ref,
    out_ref,
    cen_v, cb_v, ybuf, idbuf, ownbuf, rankbuf, send, recv, labsend, labrecv, labrow, cent, cbk, cbp, acc,
    arsend, arrecv, zsend, zrecv, finsend, finrecv,
    lsem, ysend, yrecv, isend, irecv, labs, labr, dsend, drecv, ars, arr,
):
    n_list, n_sub, n_slab, n_lists, cols, groups, codes, width = dims
    owners = n_list * n_slab
    depth = groups * width
    slots = owners * CAP
    l, y, s = lax.axis_index("list"), lax.axis_index("sub"), lax.axis_index("slab")
    me = l * n_slab + s

    cores, half = 2, n_list // 2
    far_first = sorted(range(n_slab), key=lambda d: -min(d, n_slab - d))
    slabs = [lax.rem(s + ds, n_slab) for ds in far_first]

    def wrap(v, n):
        return jnp.where(v >= n, v - n, v)

    def each_owner(do):
        def one_list(there, which):
            for w in which:
                do((there, y, slabs[w]), there * n_slab + slabs[w])

        one_list(wrap(l + half, n_list), range(n_slab))

        def two_lists(t, _):
            one_list(wrap(l + (half - t), n_list), range(n_slab))
            one_list(wrap(l + (half + t), n_list), range(n_slab))
            return 0

        lax.fori_loop(1, half, two_lists, 0)
        one_list(l, [w for w in range(n_slab) if far_first[w]])

    offs = [0]
    for d in range(1, n_sub // 2 + 1):
        offs += [d] if 2 * d == n_sub else [d, n_sub - d]

    parts = GROUPS if n_sub == 8 else tuple((r,) for r in range(n_sub))

    cen_copy = pltpu.make_async_copy(cen_ref, cen_v, lsem.at[0])
    cb_copy = pltpu.make_async_copy(cb_ref, cb_v, lsem.at[1])
    self_copy = pltpu.make_async_copy(
        vec_ref.at[pl.ds(pl.multiple_of(y * depth, depth), depth)], ybuf.at[0], lsem.at[2]
    )
    ids_copy = pltpu.make_async_copy(ids_ref, idbuf.at[0], lsem.at[3 + n_sub])
    ids_copy.start()
    self_copy.start()
    cb_copy.start()
    cen_copy.start()

    bar = pltpu.get_barrier_semaphore()
    each_owner(lambda dev, j: pl.semaphore_signal(bar, 1, device_id=dev, device_id_type=MESH))
    for d in range(1, n_sub):
        pl.semaphore_signal(bar, 1, device_id=(l, lax.rem(y + d, n_sub), s), device_id_type=MESH)


    earlier = (iota((cols, cols), 0) < iota((cols, cols), 1)).astype(BF16)

    def place(r):
        idrow = idbuf[r]
        owner = idrow // n_lists
        hit = (iota((owners, cols), 0) == owner)
        before = dot(hit.astype(BF16), earlier)
        rank = jnp.sum(jnp.where(hit, before, 0.0), axis=0, keepdims=True).astype(I32)
        number = idrow - owner * n_lists + 1
        return hit, rank, owner, number

    def rows_of(p):
        return parts[p][0] * slots, len(parts[p]) * slots

    def pack(p):
        base, count = rows_of(p)
        each = len(parts[p]) * CAP
        row = iota((count, cols), 0)
        total = None
        for i, r in enumerate(parts[p]):
            put = (row == ownbuf[r] * each + rankbuf[r] + i * CAP).astype(BF16)
            for v in split3(ybuf[r]):
                term = dot(put, v, 1, 1)
                total = term if total is None else total + term
        send[base:base + count] = total

    def send_part(p):
        base, count = rows_of(p)
        each = len(parts[p]) * CAP

        def go(dev, j):
            pltpu.make_async_remote_copy(
                src_ref=send.at[pl.ds(pl.multiple_of(base + j * each, CAP), each)],
                dst_ref=recv.at[pl.ds(pl.multiple_of(base + me * each, CAP), each)],
                send_sem=dsend.at[p], recv_sem=drecv.at[p], device_id=dev, device_id_type=MESH,
            ).start()

        each_owner(go)
        own_part(p).start()

    def own_part(p):
        base, _ = rows_of(p)
        each = len(parts[p]) * CAP
        mine = pl.ds(pl.multiple_of(base + me * each, CAP), each)
        return pltpu.make_async_copy(send.at[mine], recv.at[mine], lsem.at[3 + p])

    ids_copy.wait()
    _, rankbuf[0], ownbuf[0], _ = place(0)
    self_copy.wait()
    pack(0)

    pl.semaphore_wait(bar, owners - 1 + n_sub - 1)

    for r in range(1, n_sub):
        d = n_sub - offs[r]
        yy = lax.rem(y + d, n_sub)
        pltpu.make_async_remote_copy(
            src_ref=idbuf.at[0], dst_ref=idbuf.at[r],
            send_sem=isend, recv_sem=irecv, device_id=(l, yy, s), device_id_type=MESH,
        ).start()
    send_part(0)
    for r in range(1, n_sub):
        d = n_sub - offs[r]
        yy = lax.rem(y + d, n_sub)
        pltpu.make_async_remote_copy(
            src_ref=vec_ref.at[pl.ds(pl.multiple_of(yy * depth, depth), depth)], dst_ref=ybuf.at[r],
            send_sem=ysend, recv_sem=yrecv.at[r], device_id=(l, yy, s), device_id_type=MESH,
        ).start()

    whole = idbuf.at[pl.ds(1, n_sub - 1)]
    pltpu.make_async_copy(whole, whole, irecv).wait()
    labels = jnp.zeros((owners, 128), F32)
    for r in range(n_sub):
        hit, rank, owner, number = place(r)
        if r:
            rankbuf[r], ownbuf[r] = rank, owner
        high, low = (number // 64).astype(F32), (number % 64).astype(F32)
        q = iota((128, cols), 0) - (r * CAP)
        value = jnp.where(q == rank, high, jnp.where(q == rank + 32, low, 0.0)).astype(BF16)
        labels = labels + dot(hit.astype(BF16), value, 1, 1)
    labsend[...] = labels.reshape(owners, 1, 128)
    labrecv[me] = labsend[me]

    def send_labels(dev, j):
        pltpu.make_async_remote_copy(
            src_ref=labsend.at[j], dst_ref=labrecv.at[me],
            send_sem=labs, recv_sem=labr, device_id=dev, device_id_type=MESH,
        ).start()

    def move_on(p):
        for r in parts[p]:
            pltpu.make_async_copy(ybuf.at[r], ybuf.at[r], yrecv.at[r]).wait()
        pack(p)
        send_part(p)
        if p == 2:
            each_owner(send_labels)

    row = iota((16, slots), 0)

    def prepare(r):
        present = (labrow[r] > 0.5).astype(F32)
        arrived = recv[pl.ds(pl.multiple_of(r * slots, slots), slots)]
        return present, jnp.swapaxes(arrived, 0, 1) - cent[r]

    def sums(g, present, residual):
        part = residual[g * width:(g + 1) * width]
        r1, r2, r3 = split3(part)
        ones = jnp.where(row < 3, 1.0, 0.0).astype(BF16)
        fill = jnp.zeros((256 - 6 * width - 16, slots), BF16)
        stack = jnp.concatenate([r1, r1, r1, r2, r2, r3, ones, fill], axis=0)
        logits = dot(cbk[g], stack)
        e = jnp.exp2(logits - jnp.max(logits, axis=0, keepdims=True))
        inv = present / jnp.sum(e, axis=0, keepdims=True)
        w = jnp.concatenate([part * inv, jnp.where(row == 0, inv, 0.0)], axis=0)
        w = jnp.concatenate(split3(w), axis=0)
        e1 = e.astype(BF16)
        e2 = (e - e1.astype(F32)).astype(BF16)
        return dot(w, e1, 1, 1) + dot(w, e2, 1, 1)

    def work(r, _):
        present, residual = prepare(r)
        for g in range(groups):
            acc[g] += sums(g, present, residual)
        return 0

    def arrival(p):
        base, count = rows_of(p)
        arrived = recv.at[pl.ds(base, count - len(parts[p]) * CAP)]
        pltpu.make_async_copy(arrived, arrived, drecv.at[p]).wait()
        own_part(p).wait()

    def work_part(p):
        members = parts[p]
        arrival(p)
        if len(members) == 1:
            work(members[0], 0)
        else:
            lax.fori_loop(members[0], members[-1] + 1, work, 0)

    move_on(1)
    move_on(2)
    move_on(3)
    move_on(4)
    most = labrecv.at[pl.ds(0, owners - 1)]
    pltpu.make_async_copy(most, most, labr).wait()
    lab = labrecv[...].reshape(owners, 128).astype(BF16)
    for p, members in enumerate(parts):
        each = len(members) * CAP
        for b in range(len(members)):
            lane = iota((128, slots), 1) + b * slots
            want = lane % each + members[0] * CAP
            q = iota((128, slots), 0)
            pick = jnp.where(q == want, 64.0, jnp.where(q == want + 32, 1.0, 0.0)).astype(BF16)
            from_j = (iota((owners, slots), 1) + b * slots) // each == iota((owners, slots), 0)
            labrow[members[b]] = jnp.sum(jnp.where(from_j, dot(lab, pick), 0.0), axis=0, keepdims=True)
    cen_copy.wait()
    chunk = 512

    def gather(r, _):
        number = labrow[r].astype(I32) - 1
        total = jnp.zeros((depth, slots), F32)
        for k in range(n_lists // chunk):
            hot = (iota((chunk, slots), 0) == number - k * chunk).astype(BF16)
            total = total + dot(cen_v[:, k * chunk:(k + 1) * chunk], hot)
        cent[r] = total
        return 0

    lax.fori_loop(0, n_sub, gather, 0)

    move_on(5)
    cb_copy.wait()
    log2e = math.log2(math.e)
    for g in range(groups):
        cbt = cb_v[g]
        for h in range(codes // 128):
            cbp[g * (codes // 128) + h] = cbt[:, h * 128:h * 128 + 128]
        scaled = cbt * (2.0 / SOFTMAX_HEAT * log2e)
        norm = jnp.sum(cbt * cbt, axis=0, keepdims=True) * (-log2e / SOFTMAX_HEAT)
        c1, c2, c3 = (v.astype(F32) for v in split3(scaled))
        n1, n2, n3 = (v.astype(F32) for v in split3(norm))
        row = iota((16, codes), 0)
        tail = jnp.where(row == 0, n1, jnp.where(row == 1, n2, jnp.where(row == 2, n3, 0.0)))
        stack = jnp.concatenate([c1, c2, c3, c1, c2, c1, tail, jnp.zeros((256 - 6 * width - 16, codes), F32)], axis=0)
        cbk[g] = jnp.swapaxes(stack, 0, 1).astype(BF16)
    acc[...] = jnp.zeros_like(acc)

    work_part(0)
    work_part(1)
    work_part(2)
    work_part(3)
    work_part(4)

    z, core = l // cores, lax.rem(l, cores)
    n_z, n_k = n_list // cores, n_slab * cores
    k = s * cores + core
    rows, blocks = width + 1, codes // 128

    def along_k(i):
        to_s = lax.rem(s + i // cores, n_slab)
        to_c = lax.rem(core + i, cores)
        return (z * cores + to_c, y, to_s), to_s * cores + to_c

    order_k = sorted(range(1, n_k), key=lambda i: -min(i // cores, n_slab - i // cores))
    order_z = sorted(range(1, n_z), key=lambda i: -min(i, n_z - i))

    def give(j):
        pltpu.make_async_remote_copy(
            src_ref=arsend.at[j, pl.ds(0, rows)], dst_ref=arrecv.at[k, pl.ds(0, rows)],
            send_sem=ars.at[0], recv_sem=arr.at[0],
            device_id=(z * cores + j % cores, y, j // cores), device_id_type=MESH,
        ).start()

    for p in range(len(parts) - 1, len(parts)):
        arrival(p)
        for r in parts[p][:-1]:
            work(r, 0)
        present, residual = prepare(parts[p][-1])
        for g in range(groups):
            t = acc[g] + sums(g, present, residual)
            t = sum(t[i * (width + 16):i * (width + 16) + width + 8] for i in range(3))
            for h in range(blocks):
                j = g * blocks + h
                arsend[j] = t[:, h * 128:h * 128 + 128]
                pl.when(k != j)(functools.partial(give, j))
    arrecv[k] = arsend[k]
    got_k = arrecv.at[pl.ds(0, n_k - 1), pl.ds(0, rows)]
    pltpu.make_async_copy(got_k, got_k, arr.at[0]).wait()
    zsend[...] = jnp.sum(arrecv[...], axis=0)
    for i in order_z:
        pltpu.make_async_remote_copy(
            src_ref=zsend.at[pl.ds(0, rows)], dst_ref=zrecv.at[z, pl.ds(0, rows)],
            send_sem=ars.at[1], recv_sem=arr.at[1],
            device_id=(lax.rem(z + i, n_z) * cores + core, y, s), device_id_type=MESH,
        ).start()
    zrecv[z] = zsend[...]
    got_z = zrecv.at[pl.ds(0, n_z - 1), pl.ds(0, rows)]
    pltpu.make_async_copy(got_z, got_z, arr.at[1]).wait()
    total = jnp.sum(zrecv[...], axis=0)
    finsend[...] = (total[0:width] + PRIOR_MASS * cbp[k]) / (total[width:width + 1] + PRIOR_MASS)
    for i in order_k:
        dev, j = along_k(i)
        pltpu.make_async_remote_copy(
            src_ref=finsend, dst_ref=finrecv.at[k],
            send_sem=ars.at[2], recv_sem=arr.at[2], device_id=dev, device_id_type=MESH,
        ).start()
    finrecv[k] = finsend[...]

    pltpu.make_async_copy(whole, whole, isend).wait()
    others = ybuf.at[pl.ds(1, n_sub - 1)]
    pltpu.make_async_copy(others, others, ysend).wait()
    pltpu.make_async_copy(most, most, labs).wait()
    for p, members in enumerate(parts):
        base, count = rows_of(p)
        gone = send.at[pl.ds(base, count - len(members) * CAP)]
        pltpu.make_async_copy(gone, gone, dsend.at[p]).wait()
    pltpu.make_async_copy(got_k, got_k, ars.at[0]).wait()
    pltpu.make_async_copy(got_z, got_z, ars.at[1]).wait()

    last = finrecv.at[pl.ds(0, n_k - 1)]
    pltpu.make_async_copy(last, last, arr.at[2]).wait()
    for g in range(groups):
        for h in range(codes // 128):
            out_ref[g, :, h * 128:h * 128 + 128] = finrecv[g * (codes // 128) + h]
    pltpu.make_async_copy(last, last, ars.at[2]).wait()


def per_device(vectors, centroids, codebook, list_ids):
    n_list, n_sub, n_slab = (lax.axis_size(a) for a in ("list", "sub", "slab"))
    owners = n_list * n_slab
    n_lists, cols = centroids.shape[1], vectors.shape[1]
    groups, codes, width = codebook.shape
    depth = groups * width
    slots = owners * CAP
    n_z, n_k = n_list // 2, n_slab * 2
    dims = (n_list, n_sub, n_slab, n_lists, cols, groups, codes, width)
    dma = pltpu.SemaphoreType.DMA
    hbm = pl.BlockSpec(memory_space=pl.ANY)
    vmem = pl.BlockSpec(memory_space=pltpu.VMEM)
    out = pl.pallas_call(
        functools.partial(kernel, dims),
        out_shape=pltpu.VMEM((groups, width, codes), F32),
        in_specs=[hbm, hbm, hbm, hbm],
        out_specs=vmem,
        scratch_shapes=[
            pltpu.VMEM((depth, n_lists), BF16),
            pltpu.VMEM((groups, width, codes), F32),
            pltpu.VMEM((n_sub, depth, cols), F32),
            pltpu.VMEM((n_sub, 1, cols), I32),
            pltpu.VMEM((n_sub, 1, cols), I32),
            pltpu.VMEM((n_sub, 1, cols), I32),
            pltpu.VMEM((n_sub * slots, depth), F32),
            pltpu.VMEM((n_sub * slots, depth), F32),
            pltpu.VMEM((owners, 1, 128), F32),
            pltpu.VMEM((owners, 1, 128), F32),
            pltpu.VMEM((n_sub, 1, slots), F32),
            pltpu.VMEM((n_sub, depth, slots), F32),
            pltpu.VMEM((groups, codes, 256), BF16),
            pltpu.VMEM((n_k, width, 128), F32),
            pltpu.VMEM((groups, 3 * (width + 16), codes), F32),
            pltpu.VMEM((n_k, width + 8, 128), F32),
            pltpu.VMEM((n_k, width + 8, 128), F32),
            pltpu.VMEM((width + 8, 128), F32),
            pltpu.VMEM((n_z, width + 8, 128), F32),
            pltpu.VMEM((width, 128), F32),
            pltpu.VMEM((n_k, width, 128), F32),
            dma((4 + n_sub,)), dma, dma((n_sub,)), dma, dma, dma, dma, dma((n_sub,)), dma((n_sub,)),
            dma((3,)), dma((3,)),
        ],
        compiler_params=pltpu.CompilerParams(
            collective_id=0, has_side_effects=True, vmem_limit_bytes=60 << 20
        ),
    )(list_ids.reshape(1, cols), vectors, centroids, jnp.swapaxes(codebook, 1, 2))
    return jnp.swapaxes(out, 1, 2)


def solution(mesh):
    return jax.shard_map(
        per_device,
        mesh=mesh,
        in_specs=(
            P(None, ("list", "sub", "slab")),
            P("sub", ("list", "slab")),
            P("sub", None, None),
            P(("list", "sub", "slab")),
        ),
        out_specs=P("sub", None, None),
        check_vma=False,
    )
```
